256 devices in a mesh: seq: 8 (over x, core), res: 32 (over y, z).
Axes of the slice: x: 4, y: 4, z: 8, core: 2. Of those that a mesh axis runs over, the one named last changes fastest.
Arguments:
- alignment_matrix: bfloat16 [16, 4096, 256], P('seq', 'res'), may hold values from -400 to 400
- residue_pair_offset: bfloat16 [8, 4096, 4096], P(None, 'res'), may hold values from -400 to 400
- strand_block_filter: int32 [32, 32], replicated, may hold values from 0 to 1, as said below
- standardizer_gain: float32 [256], replicated, may hold values from 0.1 to 1.9
- combined_projection_matrix: bfloat16 [256, 1024], replicated, may hold values from -0.375 to 0.375
- final_projection_matrix: bfloat16 [256, 256], replicated, may hold values from -0.375 to 0.375
Outputs:
- columns: bfloat16 [4096, 16, 256], P(('res', 'seq'))
The draws below stay inside these ranges and needn't reach their ends.
Inputs may be any that keep to these rules, and one draw needn't show every extreme that they name: strand_block_filter[a, b] is 1 where queries of residue tile a (residues a * 128 to a * 128 + 127) may attend to keys of tile b and 0 elsewhere; it is symmetric, 1 on the diagonal, and constant over each pair of chains, a chain being a run of consecutive tiles.
All inputs are finite; a program needn't handle non-finite values.
Results may differ from the reference program's by a relative error of at most 0.0085.
Values may be sent and summed in bfloat16 or wider, within the bound.
A program may use at most 128 MiB of HBM per device.

```python
import math
import jax
import jax.numpy as jnp
from jax import lax

C = 256
H = 8
DH = 32
R_DEV = 128
S = 16
R = 4096
TILES = 32


def draw_alignment_matrix(key, part):
    key = jax.random.fold_in(key, 3)
    noise_key, row_key, col_key = jax.random.split(key, 3)
    log_span = math.log(10.0)
    row_scale = jnp.exp(jax.random.uniform(row_key, (S, R, 1), jnp.float32, 0.0, log_span))
    col_scale = jnp.exp(jax.random.uniform(col_key, (1, 1, C), jnp.float32, 0.0, log_span))
    background = jnp.clip(jax.random.normal(noise_key, (S, R, C), jnp.float32), -4.0, 4.0)
    result = background * row_scale * col_scale
    return result.astype(jnp.bfloat16)


def draw_residue_pair_offset(key, part):
    key = jax.random.fold_in(key, 7)
    noise_key = jax.random.fold_in(key, 0)
    result = jnp.clip(jax.random.normal(noise_key, (H, R, R), jnp.float32) * 2.5, -12.0, 12.0)
    return result.astype(jnp.bfloat16)


def draw_strand_block_filter(key, part):
    key = jax.random.fold_in(key, 5)
    step_key, pair_key = jax.random.split(key, 2)
    tile_ids = jnp.arange(TILES, dtype=jnp.int32)
    chain_step = jax.random.randint(step_key, (TILES,), 0, 2)
    chain_step = jnp.where(tile_ids == 0, 0, chain_step)
    chain_ids = jnp.cumsum(chain_step).astype(jnp.int32)
    pair_bits = jax.random.randint(pair_key, (TILES, TILES), 0, 2)
    row_chain = chain_ids[:, None]
    col_chain = chain_ids[None, :]
    low_chain = jnp.minimum(row_chain, col_chain)
    high_chain = jnp.maximum(row_chain, col_chain)
    linked = pair_bits[low_chain, high_chain]
    return jnp.where(row_chain == col_chain, 1, linked).astype(jnp.int32)


def centred(own_key, extent, deviation, bound, held_as=jnp.bfloat16):
    return jnp.clip(deviation * jax.random.normal(own_key, extent, jnp.float32), -bound, bound).astype(held_as)


def setup_inputs(seed: int = 0) -> dict:
    streams_of = jax.random.split(jax.random.key(seed), 7)
    return {
        "alignment_matrix": draw_alignment_matrix(jax.random.fold_in(streams_of[6], 71), 0),
        "residue_pair_offset": draw_residue_pair_offset(jax.random.fold_in(streams_of[6], 71), 0),
        "strand_block_filter": draw_strand_block_filter(jax.random.fold_in(streams_of[6], 71), 0),
        "standardizer_gain": jnp.clip(1.0 + 0.18 * jax.random.normal(streams_of[3], (C,), jnp.float32), 0.1, 1.9),
        "combined_projection_matrix": centred(streams_of[4], (C, 4 * C), C ** -0.5, 0.375),
        "final_projection_matrix": centred(streams_of[5], (C, C), C ** -0.5, 0.375),
    }


def standardize_features(values, gain):
    centered = values.astype(jnp.float32)
    row_mean = lax.optimization_barrier(jnp.mean(centered, axis=-1, keepdims=True))
    centered = centered - row_mean
    variance = lax.optimization_barrier(jnp.mean(centered * centered, axis=-1, keepdims=True))
    return centered * lax.rsqrt(variance + 1e-05) * gain.astype(jnp.float32)

def reference(alignment_matrix, residue_pair_offset, strand_block_filter, standardizer_gain, combined_projection_matrix, final_projection_matrix):
    standardized_alignment = standardize_features(alignment_matrix, standardizer_gain).astype(jnp.bfloat16)
    projected = jnp.dot(standardized_alignment.reshape(S * R, C), combined_projection_matrix, preferred_element_type=jnp.float32)
    queries = lax.optimization_barrier((projected[:, :C] * DH ** (-0.5)).astype(jnp.bfloat16)).reshape(S, R, H, DH)
    key_block = lax.optimization_barrier(projected[:, C:2 * C].astype(jnp.bfloat16)).reshape(S, R, H, DH)
    value_block = lax.optimization_barrier(projected[:, 2 * C:3 * C].astype(jnp.bfloat16)).reshape(S, R, H, DH)
    gate_logit = projected[:, 3 * C:].reshape(S, R, C)
    key_tiles = jnp.arange(R, dtype=jnp.int32) // R_DEV

    def one_block(tile_index):
        offset = tile_index * R_DEV
        query_rows = lax.dynamic_slice_in_dim(queries, offset, R_DEV, 1)
        bias_rows = lax.dynamic_slice_in_dim(residue_pair_offset, offset, R_DEV, 1)
        mask_row = lax.dynamic_index_in_dim(strand_block_filter, tile_index, 0, keepdims=False)
        allowed = jnp.take(mask_row, key_tiles) > 0

        def one_head(head_index):
            query_head = lax.dynamic_index_in_dim(query_rows, head_index, 2, keepdims=False).astype(jnp.float32)
            key_head = lax.dynamic_index_in_dim(key_block, head_index, 2, keepdims=False).astype(jnp.float32)
            value_head = lax.dynamic_index_in_dim(value_block, head_index, 2, keepdims=False).astype(jnp.float32)
            bias_head = lax.dynamic_index_in_dim(bias_rows, head_index, 0, keepdims=False).astype(jnp.float32)
            scores = jnp.einsum('sid,sjd->sij', query_head, key_head) + bias_head[None]
            row_max = lax.optimization_barrier(jnp.max(jnp.where(allowed, scores, -1e+30), axis=-1, keepdims=True))
            weights = jnp.where(allowed, jnp.exp(scores - row_max), 0.0)
            row_total = lax.optimization_barrier(jnp.sum(weights, axis=-1, keepdims=True))
            rounded = lax.optimization_barrier(weights.astype(jnp.bfloat16)).astype(jnp.float32)
            return jnp.einsum('sij,sjd->sid', rounded, value_head) / row_total
        per_head = lax.map(one_head, jnp.arange(H, dtype=jnp.int32))
        return jnp.transpose(per_head, (1, 2, 0, 3))
    per_block = lax.map(one_block, jnp.arange(TILES, dtype=jnp.int32))
    attended = jnp.transpose(per_block, (1, 0, 2, 3, 4)).reshape(S, R, C)
    gated = (jax.nn.sigmoid(gate_logit) * attended).astype(jnp.bfloat16)
    update = jnp.dot(gated.reshape(S * R, C), final_projection_matrix, preferred_element_type=jnp.float32)
    update = update.astype(jnp.bfloat16).reshape(S, R, C)
    return jnp.transpose(update, (1, 0, 2))
```

```python
import jax
import jax.numpy as jnp
from jax import lax
from jax.experimental import pallas as pl
from jax.experimental.pallas import tpu as pltpu
from jax.sharding import PartitionSpec as P

NY, NZ = 4, 8
TILES = NY * NZ
SEQ = 8
HEADS, DH, TILE, CH = 8, 32, 128, 256
ROWS = 2 * TILE
PART_A = 96
CHUNKS = (4, 4, 4, 4, 4, 4, 4, 4)
MESH = pl.DeviceIdType.MESH
BF, F32 = jnp.bfloat16, jnp.float32
NT = (((1,), (1,)), ((), ()))

SLOTS = sorted(
    ((dy, dz) for dy in (0, 1, -1, 2) for dz in (0, 1, -1, 2, -2, 3, -3, 4)),
    key=lambda d: (abs(d[0]) + abs(d[1]), abs(d[0])),
)
INDEX = {d: k for k, d in enumerate(SLOTS)}


def parent(part, slot):
    dy, dz = SLOTS[slot]
    along_z = dz != 0 if part == 0 else dy == 0
    if along_z:
        step = 1 if dz > 0 else -1
        if dz == 4 and part == 0 and dy % 2 == 1:
            step = -1
        return ("z", step), INDEX[(dy, (dz - step + 3) % NZ - 3)]
    step = 1 if dy > 0 else -1
    if dy == 2 and dz % 2 == 1:
        step = -1
    return ("y", step), INDEX[((dy - step + 1) % NY - 1, dz)]


CHILDREN = {(part, slot): [] for part in (0, 1) for slot in range(TILES)}
for _part in (0, 1):
    for _slot in range(1, TILES):
        _way, _from = parent(_part, _slot)
        CHILDREN[_part, _from].append((_way, _slot))


def chain(part, slot):
    return 1 + max([chain(part, c) for _, c in CHILDREN[part, slot]], default=0)


for _key, _list in CHILDREN.items():
    _list.sort(key=lambda e: -chain(_key[0], e[1]))


def kernel(
    x_ref, bias_ref, filter_ref, gain_ref, w_ref, wf_ref, out_ref,
    got, raw, wk, wv_t, wg_t, wf_t, keys, vals, stat, acc, mref, scores, probs, alpha, update, landed,
    send_sem, recv_sem, bias_sem, out_send, out_recv,
):
    seq, res = lax.axis_index("seq"), lax.axis_index("res")
    y, z = res // NZ, res % NZ
    near = {
        ("z", 1): y * NZ + (z + 1) % NZ,
        ("z", -1): y * NZ + (z + NZ - 1) % NZ,
        ("y", 1): ((y + 1) % NY) * NZ + z,
        ("y", -1): ((y + NY - 1) % NY) * NZ + z,
    }
    barrier = pltpu.get_barrier_semaphore()
    for other in near.values():
        pl.semaphore_signal(barrier, inc=1, device_id=(seq, other), device_id_type=MESH)
    for k in range(1, SEQ):
        pl.semaphore_signal(barrier, inc=1, device_id=((seq + k) % SEQ, res), device_id_type=MESH)

    tile_of = [((y + NY - dy) % NY) * NZ + (z + NZ - dz) % NZ for dy, dz in SLOTS]

    def bias_copy(slot):
        columns = pl.ds(pl.multiple_of(tile_of[slot] * TILE, TILE), TILE)
        return pltpu.make_async_copy(bias_ref.at[:, :, columns], raw.at[slot], bias_sem.at[slot])

    for slot in range(TILES):
        bias_copy(slot).start()

    rows = x_ref[...].reshape(ROWS, CH).astype(F32)
    rows = rows - jnp.mean(rows, axis=-1, keepdims=True)
    variance = jnp.mean(rows * rows, axis=-1, keepdims=True)
    own = (rows * lax.rsqrt(variance + 1e-5) * gain_ref[...]).astype(BF)
    got[0] = own

    pl.semaphore_wait(barrier, 4 + SEQ - 1)
    part_rows = (pl.ds(0, PART_A), pl.ds(PART_A, ROWS - PART_A))

    def block_copy(part, source, target, way):
        return pltpu.make_async_remote_copy(
            src_ref=got.at[source, part_rows[part]],
            dst_ref=got.at[target, part_rows[part]],
            send_sem=send_sem.at[target, part],
            recv_sem=recv_sem.at[target, part],
            device_id=(seq, near[way]),
            device_id_type=MESH,
        )

    started = []

    def pass_on(part, slot):
        for way, target in CHILDREN[part, slot]:
            copy = block_copy(part, slot, target, way)
            copy.start()
            started.append(copy)

    def take(part, slot):
        way, source = parent(part, slot)
        block_copy(part, source, slot, way).wait_recv()
        pass_on(part, slot)

    pass_on(0, 0)
    pass_on(1, 0)

    for part in range(2):
        for group in range(2):
            lanes = pl.ds(CH + 128 * group, 128)
            w = w_ref[:, lanes]
            if part == 1:
                w = pltpu.roll(w.astype(F32), DH, 1).astype(BF)
            wk[part, :, 128 * group : 128 * group + 128] = w
    wv_t[...] = w_ref[:, 2 * CH : 3 * CH].T
    wg_t[...] = w_ref[:, 3 * CH :].T
    wf_t[...] = wf_ref[...].T
    queries = lax.dot_general(w_ref[:, :CH].T, own, NT, preferred_element_type=F32)
    queries = (queries * DH**-0.5).astype(BF)
    unit = lax.broadcasted_iota(jnp.int32, (TILE, ROWS), 0) == lax.rem(
        lax.broadcasted_iota(jnp.int32, (TILE, ROWS), 1), TILE
    )
    unit = unit.astype(F32).astype(BF)
    for h in range(HEADS):
        first, second = DH * (h % 4), DH * ((h + 1) % 4)
        stat[h, 0:TILE, :] = jnp.zeros((TILE, ROWS), BF)
        stat[h, TILE:, :] = unit
        stat[h, first : first + DH, 0:TILE] = queries[DH * h : DH * h + DH, 0:TILE]
        stat[h, second : second + DH, TILE:] = queries[DH * h : DH * h + DH, TILE:]
        vals[h, 2 * DH :, :] = jnp.ones((16, vals.shape[2]), BF)
    acc[...] = jnp.zeros_like(acc)
    mref[...] = jnp.full(mref.shape, -1e30, F32)

    start = 0
    for index, tiles in enumerate(CHUNKS):
        if index == 0:
            for slot in range(1, tiles):
                take(0, slot)
                take(1, slot)
        size = tiles * TILE
        following = CHUNKS[index + 1] if index + 1 < len(CHUNKS) else 0
        events = [(p, s) for s in range(start + tiles, start + tiles + following) for p in (0, 1)]
        for slot in range(start, start + tiles):
            bias_copy(slot).wait()
        lane = lax.broadcasted_iota(jnp.int32, (size, 128), 1) // DH
        values = []
        for part in range(2):
            block = got[start : start + tiles, TILE * part : TILE * part + TILE].reshape(size, CH)
            keys[part, 0:size] = jnp.dot(block, wk[part], preferred_element_type=F32).astype(BF)
            values.append(
                lax.dot_general(wv_t[...], block, NT, preferred_element_type=F32).astype(BF)
            )
        for h in range(HEADS):
            for part in range(2):
                vals[h, DH * part : DH * part + DH, 0:size] = values[part][DH * h : DH * h + DH]
        closed = [
            ((1 - filter_ref[res, tile_of[slot]]).astype(F32) * -1e30).astype(BF)
            for slot in range(start, start + tiles)
        ]

        def score(h):
            lanes = slice(128 * (h // 4), 128 * (h // 4) + 128)
            key = jnp.where(lane == h % 4, keys[0, 0:size, lanes], keys[1, 0:size, lanes])
            offset = jnp.concatenate(
                [raw[start + t, h].T + closed[t] for t in range(tiles)], axis=0
            )
            scores[h % 2, 0:size] = jnp.dot(
                jnp.concatenate([key, offset], axis=1), stat[h], preferred_element_type=F32
            )

        def weigh(h):
            old = mref[h]
            new = jnp.maximum(old, jnp.max(scores[h % 2, 0:size], axis=0, keepdims=True))
            alpha[h] = jnp.exp(old - new)
            mref[h] = new
            probs[h % 2, 0:size] = jnp.exp(scores[h % 2, 0:size] - new[0:1]).astype(BF)

        def add(h):
            acc[h] = acc[h] * alpha[h, 0:1] + jnp.dot(
                vals[h, :, 0:size], probs[h % 2, 0:size], preferred_element_type=F32
            )

        for step in range(HEADS + 2):
            if step < HEADS:
                score(step)
            if 0 <= step - 1 < HEADS:
                weigh(step - 1)
            if 0 <= step - 2 < HEADS:
                add(step - 2)
            if step in EVENT_STEPS:
                k = EVENT_STEPS.index(step)
                n = len(EVENT_STEPS)
                for event in events[len(events) * k // n : len(events) * (k + 1) // n]:
                    take(*event)
        start += tiles

    gate = lax.dot_general(wg_t[...], own, NT, preferred_element_type=F32)
    attended = []
    for h in range(HEADS):
        inverse = 1.0 / acc[h, 2 * DH : 2 * DH + 1, :]
        attended.append(
            jnp.concatenate(
                [
                    acc[h, 0:DH, 0:TILE] * inverse[:, 0:TILE],
                    acc[h, DH : 2 * DH, TILE:] * inverse[:, TILE:],
                ],
                axis=1,
            )
        )
    gated = (jax.nn.sigmoid(gate) * jnp.concatenate(attended, axis=0)).astype(BF)
    new = jnp.dot(wf_t[...], gated, preferred_element_type=F32)
    update[...] = new.T.astype(BF).reshape(2, TILE, CH)

    share = TILE // SEQ

    def share_of(owner):
        return update.at[:, pl.ds(pl.multiple_of(owner * share, share), share)]

    sent = []
    for k in range(1, SEQ):
        owner = (seq + k) % SEQ
        copy = pltpu.make_async_remote_copy(
            src_ref=share_of(owner),
            dst_ref=landed.at[seq],
            send_sem=out_send.at[k],
            recv_sem=out_recv.at[k],
            device_id=(owner, res),
            device_id_type=MESH,
        )
        copy.start()
        sent.append(copy)
    mine = pltpu.make_async_copy(share_of(seq), landed.at[seq], out_recv.at[0])
    mine.start()
    for copy in started:
        copy.wait_send()
    mine.wait()
    for copy in sent:
        copy.wait()
    out_ref[...] = landed[...].reshape(2 * SEQ, share, CH)


EVENT_STEPS = (0, 1, 2, 3, 4, 5, 6, 7)


def on_device(x, bias, allowed, gain, w, wf):
    vmem = pl.BlockSpec(memory_space=pltpu.VMEM)
    longest = max(CHUNKS) * TILE
    out = pl.pallas_call(
        kernel,
        out_shape=jax.ShapeDtypeStruct((2 * SEQ, TILE // SEQ, CH), BF),
        in_specs=[
            vmem,
            pl.BlockSpec(memory_space=pl.ANY),
            pl.BlockSpec(memory_space=pltpu.SMEM),
            vmem,
            vmem,
            vmem,
        ],
        out_specs=vmem,
        scratch_shapes=[
            pltpu.VMEM((TILES, ROWS, CH), BF),
            pltpu.VMEM((TILES, HEADS, TILE, TILE), BF),
            pltpu.VMEM((2, CH, CH), BF),
            pltpu.VMEM((CH, CH), BF),
            pltpu.VMEM((CH, CH), BF),
            pltpu.VMEM((CH, CH), BF),
            pltpu.VMEM((2, longest, CH), BF),
            pltpu.VMEM((HEADS, 2 * DH + 16, longest), BF),
            pltpu.VMEM((HEADS, 2 * TILE, ROWS), BF),
            pltpu.VMEM((HEADS, 2 * DH + 16, ROWS), F32),
            pltpu.VMEM((HEADS, 8, ROWS), F32),
            pltpu.VMEM((2, longest, ROWS), F32),
            pltpu.VMEM((2, longest, ROWS), BF),
            pltpu.VMEM((HEADS, 8, ROWS), F32),
            pltpu.VMEM((2, TILE, CH), BF),
            pltpu.VMEM((SEQ, 2, TILE // SEQ, CH), BF),
            pltpu.SemaphoreType.DMA((TILES, 2)),
            pltpu.SemaphoreType.DMA((TILES, 2)),
            pltpu.SemaphoreType.DMA((TILES,)),
            pltpu.SemaphoreType.DMA((SEQ,)),
            pltpu.SemaphoreType.DMA((SEQ,)),
        ],
        compiler_params=pltpu.CompilerParams(
            collective_id=0, has_side_effects=True, vmem_limit_bytes=40 * 2**20
        ),
        cost_estimate=pl.CostEstimate(
            flops=4 * 2**30, bytes_accessed=9 * 2**20, transcendentals=2**23
        ),
    )(x, bias, allowed, gain.reshape(1, CH), w, wf)
    return jnp.transpose(out, (1, 0, 2))


def solution(mesh):
    return jax.shard_map(
        on_device,
        mesh=mesh,
        in_specs=(P("seq", "res", None), P(None, "res", None), P(), P(), P(), P()),
        out_specs=P(("res", "seq"), None, None),
        check_vma=False,
    )
```

```python
import jax
import jax.numpy as jnp
from jax import lax
from jax.experimental import pallas as pl
from jax.experimental.pallas import tpu as pltpu
from jax.sharding import PartitionSpec as P

NY, NZ = 4, 8
TILES = NY * NZ
SEQ = 8
HEADS, DH, TILE, CH = 8, 32, 128, 256
ROWS = 2 * TILE
PARTS = (96, 80, 80)
CHUNKS = (4, 4, 4, 4, 4, 4, 4, 3, 1)
MESH = pl.DeviceIdType.MESH
BF, F32 = jnp.bfloat16, jnp.float32
NT = (((1,), (1,)), ((), ()))

SLOTS = (
    (0, 0), (1, 0), (-1, 0), (0, 1), (0, -1), (-1, -1), (-1, 1), (1, -1), (1, 1), (0, 2), (0, -2), (2, 0),
    (-1, 2), (2, -1), (-1, -2), (1, -2), (0, 3), (2, 1), (1, 2), (0, -3), (-1, 3), (2, 2), (0, 4), (2, -2),
    (1, 3), (-1, -3), (2, 3), (-1, 4), (1, 4), (1, -3), (2, -3), (2, 4),
)

SEND, TAKE, PREPARE, ATTEND = range(4)
PLAN = (
    (0, 0, 0, 1), (0, 0, 0, 2), (0, 1, 0, 3), (0, 2, 0, 4), (2,), (0, 2, 0, 1), (0, 1, 0, 2), (0, 2, 0, 3),
    (0, 1, 0, 4), (0, 1, 0, 1), (0, 2, 0, 2), (0, 0, 0, 3), (0, 0, 0, 4), (1, 1, 3), (1, 2, 4), (0, 2, 4, 7),
    (0, 1, 3, 6), (0, 1, 3, 9), (0, 2, 4, 10), (0, 1, 3, 8), (0, 2, 4, 5), (1, 0, 1), (1, 0, 2), (0, 0, 2, 6),
    (0, 0, 2, 5), (0, 0, 1, 11), (1, 2, 1), (1, 1, 2), (1, 2, 3), (1, 1, 4), (0, 1, 4, 5), (0, 2, 3, 9),
    (0, 0, 1, 7), (0, 2, 3, 6), (0, 1, 4, 7), (1, 1, 1), (1, 2, 2), (0, 0, 1, 8), (1, 0, 3), (1, 0, 4),
    (0, 1, 4, 10), (0, 2, 3, 8), (0, 2, 2, 11), (0, 0, 3, 9), (0, 0, 4, 10), (3, 0, 0, 4), (1, 2, 7),
    (1, 1, 6), (1, 1, 9), (1, 2, 10), (0, 1, 9, 12), (0, 2, 7, 13), (0, 1, 6, 17), (0, 1, 9, 16),
    (0, 2, 10, 19), (0, 1, 1, 11), (3, 0, 4, 8), (1, 1, 8), (1, 2, 5), (1, 0, 6), (1, 0, 5), (0, 0, 6, 12),
    (0, 0, 5, 14), (1, 1, 5), (1, 0, 11), (1, 2, 9), (0, 1, 5, 13), (0, 2, 9, 18), (1, 0, 7), (1, 2, 6),
    (0, 2, 9, 16), (0, 0, 7, 15), (1, 1, 7), (0, 2, 10, 15), (0, 2, 9, 12), (0, 0, 11, 17), (0, 0, 11, 13),
    (0, 1, 9, 18), (0, 2, 10, 14), (3, 1, 0, 4), (1, 0, 8), (1, 1, 10), (1, 2, 11), (1, 2, 8), (1, 0, 9),
    (1, 0, 10), (0, 1, 10, 15), (0, 1, 10, 14), (0, 0, 9, 16), (0, 1, 10, 19), (3, 1, 4, 8), (1, 1, 12),
    (1, 2, 13), (1, 1, 16), (1, 2, 19), (1, 1, 17), (1, 1, 11), (0, 2, 19, 29), (0, 1, 16, 20),
    (0, 1, 16, 22), (0, 2, 19, 22), (0, 2, 8, 17), (0, 2, 19, 25), (0, 0, 8, 18), (0, 0, 10, 19),
    (3, 2, 0, 4), (1, 0, 12), (1, 0, 14), (1, 1, 13), (1, 2, 18), (1, 2, 16), (1, 2, 12), (1, 0, 15),
    (1, 2, 15), (0, 2, 16, 20), (0, 2, 16, 24), (0, 1, 16, 24), (0, 2, 12, 21), (0, 0, 12, 20),
    (0, 0, 15, 29), (3, 2, 4, 8), (1, 2, 14), (1, 0, 17), (1, 1, 18), (1, 0, 13), (0, 0, 17, 21),
    (0, 0, 14, 25), (1, 1, 14), (1, 1, 15), (0, 1, 18, 21), (0, 2, 14, 23), (0, 0, 13, 23), (0, 1, 15, 23),
    (3, 3, 0, 4), (1, 0, 16), (1, 1, 19), (1, 1, 20), (1, 2, 29), (1, 1, 22), (1, 2, 22), (0, 1, 22, 27),
    (0, 0, 16, 22), (0, 1, 22, 28), (0, 1, 20, 26), (3, 3, 4, 8), (1, 2, 25), (1, 2, 17), (1, 0, 18),
    (1, 0, 19), (1, 2, 20), (1, 2, 24), (0, 1, 19, 25), (0, 0, 18, 24), (0, 2, 24, 26), (0, 2, 29, 30),
    (0, 2, 22, 27), (3, 4, 0, 4), (1, 0, 20), (1, 0, 29), (1, 2, 21), (1, 1, 24), (1, 0, 21), (1, 0, 25),
    (1, 2, 23), (0, 0, 21, 26), (0, 0, 25, 27), (1, 1, 21), (0, 2, 22, 28), (0, 0, 29, 28), (0, 1, 19, 29),
    (3, 4, 4, 8), (1, 1, 27), (1, 0, 22), (1, 0, 23), (1, 1, 23), (0, 0, 23, 30), (3, 5, 0, 4), (1, 1, 26),
    (1, 1, 28), (1, 0, 24), (0, 1, 28, 31), (1, 1, 25), (0, 1, 25, 30), (3, 5, 4, 8), (1, 2, 26), (1, 2, 27),
    (1, 0, 26), (1, 2, 30), (1, 0, 27), (0, 2, 27, 31), (0, 0, 26, 31), (3, 6, 0, 4), (1, 2, 28), (1, 0, 28),
    (3, 6, 4, 8), (1, 1, 29), (1, 0, 30), (1, 1, 30), (3, 7, 0, 4), (1, 1, 31), (3, 7, 4, 8), (1, 2, 31),
    (1, 0, 31), (3, 8, 0, 4), (3, 8, 4, 8),
)


def way_of(source, target):
    dy = (SLOTS[target][0] - SLOTS[source][0]) % NY
    dz = (SLOTS[target][1] - SLOTS[source][1]) % NZ
    return ("y", 1 if dy == 1 else -1) if dy else ("z", 1 if dz == 1 else -1)


FROM = {(step[1], step[3]): step[2] for step in PLAN if step[0] == SEND}


def kernel(
    x_hbm, bias_ref, filter_hbm, gain_hbm, w_hbm, wf_hbm, out_ref,
    x_ref, filter_ref, gain_ref, w_ref, wf_ref, got, raw, wk, wv_t, gate_ref, wf_t, keys, vals, stat, acc, mref, scores, probs, alpha, update, landed,
    load_sem, send_sem, recv_sem, bias_sem, out_send, out_recv,
):
    seq, res = lax.axis_index("seq"), lax.axis_index("res")
    y, z = res // NZ, res % NZ
    near = {
        ("z", 1): y * NZ + (z + 1) % NZ,
        ("z", -1): y * NZ + (z + NZ - 1) % NZ,
        ("y", 1): ((y + 1) % NY) * NZ + z,
        ("y", -1): ((y + NY - 1) % NY) * NZ + z,
    }
    loads = [
        pltpu.make_async_copy(source, target, load_sem.at[k])
        for k, (source, target) in enumerate(
            (
                (x_hbm, x_ref),
                (gain_hbm, gain_ref),
                (w_hbm, w_ref),
                (wf_hbm, wf_ref),
                (filter_hbm, filter_ref),
            )
        )
    ]
    for load in loads:
        load.start()
    barrier = pltpu.get_barrier_semaphore()
    for other in near.values():
        pl.semaphore_signal(barrier, inc=1, device_id=(seq, other), device_id_type=MESH)
    for k in range(1, SEQ):
        pl.semaphore_signal(barrier, inc=1, device_id=((seq + k) % SEQ, res), device_id_type=MESH)

    tile_of = [((y + NY - dy) % NY) * NZ + (z + NZ - dz) % NZ for dy, dz in SLOTS]

    def bias_copy(slot):
        columns = pl.ds(pl.multiple_of(tile_of[slot] * TILE, TILE), TILE)
        return pltpu.make_async_copy(bias_ref.at[:, :, columns], raw.at[slot], bias_sem.at[slot])

    for slot in range(TILES):
        bias_copy(slot).start()

    loads[0].wait()
    loads[1].wait()
    rows = x_ref[...].reshape(ROWS, CH).astype(F32)
    rows = rows - jnp.mean(rows, axis=-1, keepdims=True)
    variance = jnp.mean(rows * rows, axis=-1, keepdims=True)
    own = (rows * lax.rsqrt(variance + 1e-5) * gain_ref[...]).astype(BF)
    got[0] = own

    pl.semaphore_wait(barrier, 4 + SEQ - 1)
    part_rows = [pl.ds(sum(PARTS[:k]), PARTS[k]) for k in range(len(PARTS))]

    def block_copy(part, source, target):
        return pltpu.make_async_remote_copy(
            src_ref=got.at[source, part_rows[part]],
            dst_ref=got.at[target, part_rows[part]],
            send_sem=send_sem.at[target, part],
            recv_sem=recv_sem.at[target, part],
            device_id=(seq, near[way_of(source, target)]),
            device_id_type=MESH,
        )

    def prepare():
        for load in loads[2:]:
            load.wait()
        for part in range(2):
            for group in range(2):
                lanes = pl.ds(CH + 128 * group, 128)
                w = w_ref[:, lanes]
                if part == 1:
                    w = pltpu.roll(w.astype(F32), DH, 1).astype(BF)
                wk[part, :, 128 * group : 128 * group + 128] = w
        wv_t[...] = w_ref[:, 2 * CH : 3 * CH].T
        wf_t[...] = wf_ref[...].T
        queries = lax.dot_general(w_ref[:, :CH].T, own, NT, preferred_element_type=F32)
        queries = (queries * DH**-0.5).astype(BF)
        unit = lax.broadcasted_iota(jnp.int32, (TILE, ROWS), 0) == lax.rem(
            lax.broadcasted_iota(jnp.int32, (TILE, ROWS), 1), TILE
        )
        unit = unit.astype(F32).astype(BF)
        for h in range(HEADS):
            first, second = DH * (h % 4), DH * ((h + 1) % 4)
            stat[h, 0:TILE, :] = jnp.zeros((TILE, ROWS), BF)
            stat[h, TILE:, :] = unit
            stat[h, first : first + DH, 0:TILE] = queries[DH * h : DH * h + DH, 0:TILE]
            stat[h, second : second + DH, TILE:] = queries[DH * h : DH * h + DH, TILE:]
            for half in range(2):
                vals[half, h, 2 * DH :, :] = jnp.ones((16, vals.shape[3]), BF)
        gate_ref[...] = jax.nn.sigmoid(
            lax.dot_general(w_ref[:, 3 * CH :].T, own, NT, preferred_element_type=F32)
        )
        acc[...] = jnp.zeros_like(acc)
        mref[...] = jnp.full(mref.shape, -1e30, F32)

    first = [sum(CHUNKS[:k]) for k in range(len(CHUNKS) + 1)]

    def slots_of(chunk):
        return range(first[chunk], first[chunk + 1])

    def project_keys(chunk):
        size = CHUNKS[chunk] * TILE
        for part in range(2):
            block = got[first[chunk] : first[chunk + 1], TILE * part : TILE * part + TILE]
            block = block.reshape(size, CH)
            keys[part, 0:size] = jnp.dot(block, wk[part], preferred_element_type=F32).astype(BF)

    def project_values(chunk):
        size = CHUNKS[chunk] * TILE
        for part in range(2):
            block = got[first[chunk] : first[chunk + 1], TILE * part : TILE * part + TILE]
            block = block.reshape(size, CH)
            value = lax.dot_general(wv_t[...], block, NT, preferred_element_type=F32).astype(BF)
            for h in range(HEADS):
                vals[chunk % 2, h, DH * part : DH * part + DH, 0:size] = value[
                    DH * h : DH * h + DH
                ]

    def score(chunk, h):
        size = CHUNKS[chunk] * TILE
        lane = lax.broadcasted_iota(jnp.int32, (size, 128), 1) // DH
        lanes = slice(128 * (h // 4), 128 * (h // 4) + 128)
        key = jnp.where(lane == h % 4, keys[0, 0:size, lanes], keys[1, 0:size, lanes])
        offset = []
        for slot in slots_of(chunk):
            closed = (1 - filter_ref[res, tile_of[slot]]).astype(F32) * -1e30
            offset.append(raw[slot, h].T + closed.astype(BF))
        scores[h % 2, 0:size] = jnp.dot(
            jnp.concatenate([key, jnp.concatenate(offset, axis=0)], axis=1),
            stat[h],
            preferred_element_type=F32,
        )

    def weigh(chunk, h):
        size = CHUNKS[chunk] * TILE
        old = mref[h]
        new = jnp.maximum(old, jnp.max(scores[h % 2, 0:size], axis=0, keepdims=True))
        alpha[h] = jnp.exp(old - new)
        mref[h] = new
        probs[h % 2, 0:size] = jnp.exp(scores[h % 2, 0:size] - new[0:1]).astype(BF)

    def add(chunk, h):
        size = CHUNKS[chunk] * TILE
        acc[h] = acc[h] * alpha[h, 0:1] + jnp.dot(
            vals[chunk % 2, h, :, 0:size], probs[h % 2, 0:size], preferred_element_type=F32
        )

    work = []

    def advance(item):
        work.append(item)
        if item is not None:
            chunk, h = item
            if h == 0:
                for slot in slots_of(chunk):
                    bias_copy(slot).wait()
                project_keys(chunk)
            score(chunk, h)
            if h == 0:
                project_values(chunk)
        if len(work) > 1 and work[-2] is not None:
            weigh(*work[-2])
        if len(work) > 2:
            add(*work[-3])

    started = []
    for step in PLAN:
        if step[0] == SEND:
            copy = block_copy(*step[1:])
            copy.start()
            started.append(copy)
        elif step[0] == TAKE:
            block_copy(step[1], FROM[step[1:]], step[2]).wait_recv()
        elif step[0] == PREPARE:
            prepare()
        else:
            for h in range(step[2], step[3]):
                advance((step[1], h))
    advance(None)
    advance(None)

    attended = []
    for h in range(HEADS):
        inverse = 1.0 / acc[h, 2 * DH : 2 * DH + 1, :]
        attended.append(
            jnp.concatenate(
                [
                    acc[h, 0:DH, 0:TILE] * inverse[:, 0:TILE],
                    acc[h, DH : 2 * DH, TILE:] * inverse[:, TILE:],
                ],
                axis=1,
            )
        )
    gated = (gate_ref[...] * jnp.concatenate(attended, axis=0)).astype(BF)
    new = jnp.dot(wf_t[...], gated, preferred_element_type=F32)
    update[...] = new.T.astype(BF).reshape(2, TILE, CH)

    share = TILE // SEQ

    def share_of(owner):
        return update.at[:, pl.ds(pl.multiple_of(owner * share, share), share)]

    sent = []
    for k in range(1, SEQ):
        owner = (seq + k) % SEQ
        copy = pltpu.make_async_remote_copy(
            src_ref=share_of(owner),
            dst_ref=landed.at[seq],
            send_sem=out_send.at[k],
            recv_sem=out_recv.at[k],
            device_id=(owner, res),
            device_id_type=MESH,
        )
        copy.start()
        sent.append(copy)
    mine = pltpu.make_async_copy(share_of(seq), landed.at[seq], out_recv.at[0])
    mine.start()
    for copy in started:
        copy.wait_send()
    mine.wait()
    for copy in sent:
        copy.wait()
    out_ref[...] = landed[...].reshape(2 * SEQ, share, CH)


def on_device(x, bias, allowed, gain, w, wf):
    vmem = pl.BlockSpec(memory_space=pltpu.VMEM)
    longest = max(CHUNKS) * TILE
    out = pl.pallas_call(
        kernel,
        out_shape=jax.ShapeDtypeStruct((2 * SEQ, TILE // SEQ, CH), BF),
        in_specs=[pl.BlockSpec(memory_space=pltpu.HBM)] * 6,
        out_specs=vmem,
        scratch_shapes=[
            pltpu.VMEM((2, TILE, CH), BF),
            pltpu.SMEM((TILES, TILES), jnp.int32),
            pltpu.VMEM((1, CH), F32),
            pltpu.VMEM((CH, 4 * CH), BF),
            pltpu.VMEM((CH, CH), BF),
            pltpu.VMEM((TILES, ROWS, CH), BF),
            pltpu.VMEM((TILES, HEADS, TILE, TILE), BF),
            pltpu.VMEM((2, CH, CH), BF),
            pltpu.VMEM((CH, CH), BF),
            pltpu.VMEM((CH, ROWS), F32),
            pltpu.VMEM((CH, CH), BF),
            pltpu.VMEM((2, longest, CH), BF),
            pltpu.VMEM((2, HEADS, 2 * DH + 16, longest), BF),
            pltpu.VMEM((HEADS, 2 * TILE, ROWS), BF),
            pltpu.VMEM((HEADS, 2 * DH + 16, ROWS), F32),
            pltpu.VMEM((HEADS, 8, ROWS), F32),
            pltpu.VMEM((2, longest, ROWS), F32),
            pltpu.VMEM((2, longest, ROWS), BF),
            pltpu.VMEM((HEADS, 8, ROWS), F32),
            pltpu.VMEM((2, TILE, CH), BF),
            pltpu.VMEM((SEQ, 2, TILE // SEQ, CH), BF),
            pltpu.SemaphoreType.DMA((5,)),
            pltpu.SemaphoreType.DMA((TILES, len(PARTS))),
            pltpu.SemaphoreType.DMA((TILES, len(PARTS))),
            pltpu.SemaphoreType.DMA((TILES,)),
            pltpu.SemaphoreType.DMA((SEQ,)),
            pltpu.SemaphoreType.DMA((SEQ,)),
        ],
        compiler_params=pltpu.CompilerParams(
            collective_id=0, has_side_effects=True, vmem_limit_bytes=63 * 2**20
        ),
        cost_estimate=pl.CostEstimate(
            flops=4 * 2**30, bytes_accessed=9 * 2**20, transcendentals=2**23
        ),
    )(x, bias, allowed, gain.reshape(1, CH), w, wf)
    return jnp.transpose(out, (1, 0, 2))


def solution(mesh):
    return jax.shard_map(
        on_device,
        mesh=mesh,
        in_specs=(P("seq", "res", None), P(None, "res", None), P(), P(), P(), P()),
        out_specs=P(("res", "seq"), None, None),
        check_vma=False,
    )
```

```python
import jax
import jax.numpy as jnp
from jax import lax
from jax.experimental import pallas as pl
from jax.experimental.pallas import tpu as pltpu
from jax.sharding import PartitionSpec as P

NY, NZ = 4, 8
TILES = NY * NZ
SEQ = 8
HEADS, DH, TILE, CH = 8, 32, 128, 256
ROWS = 2 * TILE
PARTS = (96, 80, 80)
CHUNKS = (4, 4, 4, 4, 4, 4, 4, 3, 1)
MESH = pl.DeviceIdType.MESH
BF, F32 = jnp.bfloat16, jnp.float32
NT = (((1,), (1,)), ((), ()))
TN = (((0,), (0,)), ((), ()))

SLOTS = (
    (0, 0), (1, 0), (-1, 0), (0, 1), (0, -1), (-1, -1), (-1, 1), (1, -1), (1, 1), (0, 2), (0, -2), (2, 0),
    (-1, 2), (2, -1), (-1, -2), (1, -2), (0, 3), (2, 1), (1, 2), (0, -3), (-1, 3), (2, 2), (0, 4), (2, -2),
    (1, 3), (-1, -3), (2, 3), (-1, 4), (1, 4), (1, -3), (2, -3), (2, 4),
)

SEND, TAKE, PREPARE, ATTEND = range(4)
PLAN = (
    (0, 0, 0, 1), (0, 0, 0, 2), (0, 1, 0, 3), (0, 2, 0, 4), (2,), (0, 2, 0, 1), (0, 1, 0, 2), (0, 2, 0, 3),
    (0, 1, 0, 4), (0, 1, 0, 1), (0, 2, 0, 2), (0, 0, 0, 3), (0, 0, 0, 4), (1, 1, 3), (1, 2, 4), (0, 2, 4, 7),
    (0, 1, 3, 6), (0, 1, 3, 9), (0, 2, 4, 10), (0, 1, 3, 8), (0, 2, 4, 5), (1, 0, 1), (1, 0, 2), (0, 0, 2, 6),
    (0, 0, 2, 5), (0, 0, 1, 11), (1, 2, 1), (1, 1, 2), (1, 2, 3), (1, 1, 4), (0, 1, 4, 5), (0, 2, 3, 9),
    (0, 0, 1, 7), (0, 2, 3, 6), (0, 1, 4, 7), (1, 1, 1), (1, 2, 2), (0, 0, 1, 8), (1, 0, 3), (1, 0, 4),
    (0, 1, 4, 10), (0, 2, 3, 8), (0, 2, 2, 11), (0, 0, 3, 9), (0, 0, 4, 10), (3, 0, 0, 4), (1, 2, 7),
    (1, 1, 6), (1, 1, 9), (1, 2, 10), (0, 1, 9, 12), (0, 2, 7, 13), (0, 1, 6, 17), (0, 1, 9, 16),
    (0, 2, 10, 19), (0, 1, 1, 11), (3, 0, 4, 8), (1, 1, 8), (1, 2, 5), (1, 0, 6), (1, 0, 5), (0, 0, 6, 12),
    (0, 0, 5, 14), (1, 1, 5), (1, 0, 11), (1, 2, 9), (0, 1, 5, 13), (0, 2, 9, 18), (1, 0, 7), (1, 2, 6),
    (0, 2, 9, 16), (0, 0, 7, 15), (1, 1, 7), (0, 2, 10, 15), (0, 2, 9, 12), (0, 0, 11, 17), (0, 0, 11, 13),
    (0, 1, 9, 18), (0, 2, 10, 14), (3, 1, 0, 4), (1, 0, 8), (1, 1, 10), (1, 2, 11), (1, 2, 8), (1, 0, 9),
    (1, 0, 10), (0, 1, 10, 15), (0, 1, 10, 14), (0, 0, 9, 16), (0, 1, 10, 19), (3, 1, 4, 8), (1, 1, 12),
    (1, 2, 13), (1, 1, 16), (1, 2, 19), (1, 1, 17), (1, 1, 11), (0, 2, 19, 29), (0, 1, 16, 20),
    (0, 1, 16, 22), (0, 2, 19, 22), (0, 2, 8, 17), (0, 2, 19, 25), (0, 0, 8, 18), (0, 0, 10, 19),
    (3, 2, 0, 4), (1, 0, 12), (1, 0, 14), (1, 1, 13), (1, 2, 18), (1, 2, 16), (1, 2, 12), (1, 0, 15),
    (1, 2, 15), (0, 2, 16, 20), (0, 2, 16, 24), (0, 1, 16, 24), (0, 2, 12, 21), (0, 0, 12, 20),
    (0, 0, 15, 29), (3, 2, 4, 8), (1, 2, 14), (1, 0, 17), (1, 1, 18), (1, 0, 13), (0, 0, 17, 21),
    (0, 0, 14, 25), (1, 1, 14), (1, 1, 15), (0, 1, 18, 21), (0, 2, 14, 23), (0, 0, 13, 23), (0, 1, 15, 23),
    (3, 3, 0, 4), (1, 0, 16), (1, 1, 19), (1, 1, 20), (1, 2, 29), (1, 1, 22), (1, 2, 22), (0, 1, 22, 27),
    (0, 0, 16, 22), (0, 1, 22, 28), (0, 1, 20, 26), (3, 3, 4, 8), (1, 2, 25), (1, 2, 17), (1, 0, 18),
    (1, 0, 19), (1, 2, 20), (1, 2, 24), (0, 1, 19, 25), (0, 0, 18, 24), (0, 2, 24, 26), (0, 2, 29, 30),
    (0, 2, 22, 27), (3, 4, 0, 4), (1, 0, 20), (1, 0, 29), (1, 2, 21), (1, 1, 24), (1, 0, 21), (1, 0, 25),
    (1, 2, 23), (0, 0, 21, 26), (0, 0, 25, 27), (1, 1, 21), (0, 2, 22, 28), (0, 0, 29, 28), (0, 1, 19, 29),
    (3, 4, 4, 8), (1, 1, 27), (1, 0, 22), (1, 0, 23), (1, 1, 23), (0, 0, 23, 30), (3, 5, 0, 4), (1, 1, 26),
    (1, 1, 28), (1, 0, 24), (0, 1, 28, 31), (1, 1, 25), (0, 1, 25, 30), (3, 5, 4, 8), (1, 2, 26), (1, 2, 27),
    (1, 0, 26), (1, 2, 30), (1, 0, 27), (0, 2, 27, 31), (0, 0, 26, 31), (3, 6, 0, 4), (1, 2, 28), (1, 0, 28),
    (3, 6, 4, 8), (1, 1, 29), (1, 0, 30), (1, 1, 30), (3, 7, 0, 4), (1, 1, 31), (3, 7, 4, 8), (1, 2, 31),
    (1, 0, 31), (3, 8, 0, 4), (3, 8, 4, 8),
)


def way_of(source, target):
    dy = (SLOTS[target][0] - SLOTS[source][0]) % NY
    dz = (SLOTS[target][1] - SLOTS[source][1]) % NZ
    return ("y", 1 if dy == 1 else -1) if dy else ("z", 1 if dz == 1 else -1)


FROM = {(step[1], step[3]): step[2] for step in PLAN if step[0] == SEND}


def kernel(
    x_hbm, bias_ref, filter_hbm, gain_hbm, w_hbm, wf_hbm, out_ref,
    x_ref, filter_ref, gain_ref, w_ref, wf_ref, got, raw, wk, wv_t, gate_ref, keys, vals, stat, acc, mref, scores, probs, alpha, update,
    load_sem, send_sem, recv_sem, bias_sem, out_send, out_recv,
):
    seq, res = lax.axis_index("seq"), lax.axis_index("res")
    y, z = res // NZ, res % NZ
    near = {
        ("z", 1): y * NZ + (z + 1) % NZ,
        ("z", -1): y * NZ + (z + NZ - 1) % NZ,
        ("y", 1): ((y + 1) % NY) * NZ + z,
        ("y", -1): ((y + NY - 1) % NY) * NZ + z,
    }
    barrier = pltpu.get_barrier_semaphore()
    for other in near.values():
        pl.semaphore_signal(barrier, inc=1, device_id=(seq, other), device_id_type=MESH)
    for k in range(1, SEQ):
        pl.semaphore_signal(barrier, inc=1, device_id=((seq + k) % SEQ, res), device_id_type=MESH)

    loads = [
        pltpu.make_async_copy(source, target, load_sem.at[k])
        for k, (source, target) in enumerate(
            (
                (x_hbm, x_ref),
                (gain_hbm, gain_ref),
                (w_hbm, w_ref),
                (wf_hbm, wf_ref),
                (filter_hbm, filter_ref),
            )
        )
    ]
    for load in loads:
        load.start()
    tile_of = [((y + NY - dy) % NY) * NZ + (z + NZ - dz) % NZ for dy, dz in SLOTS]

    def bias_copy(slot):
        columns = pl.ds(pl.multiple_of(tile_of[slot] * TILE, TILE), TILE)
        return pltpu.make_async_copy(bias_ref.at[:, :, columns], raw.at[slot], bias_sem.at[slot])

    loads[0].wait()
    loads[1].wait()
    rows = x_ref[...].reshape(ROWS, CH).astype(F32)
    rows = rows - jnp.mean(rows, axis=-1, keepdims=True)
    variance = jnp.mean(rows * rows, axis=-1, keepdims=True)
    own = (rows * lax.rsqrt(variance + 1e-5) * gain_ref[...]).astype(BF)
    got[0] = own

    pl.semaphore_wait(barrier, 4 + SEQ - 1)
    part_rows = [pl.ds(sum(PARTS[:k]), PARTS[k]) for k in range(len(PARTS))]

    def block_copy(part, source, target):
        return pltpu.make_async_remote_copy(
            src_ref=got.at[source, part_rows[part]],
            dst_ref=got.at[target, part_rows[part]],
            send_sem=send_sem.at[target, part],
            recv_sem=recv_sem.at[target, part],
            device_id=(seq, near[way_of(source, target)]),
            device_id_type=MESH,
        )

    def prepare():
        for slot in range(TILES):
            bias_copy(slot).start()
        for load in loads[2:]:
            load.wait()
        for part in range(2):
            for group in range(2):
                lanes = pl.ds(CH + 128 * group, 128)
                w = w_ref[:, lanes]
                if part == 1:
                    w = pltpu.roll(w.astype(F32), DH, 1).astype(BF)
                wk[part, :, 128 * group : 128 * group + 128] = w
        wv_t[...] = w_ref[:, 2 * CH : 3 * CH].T
        queries = lax.dot_general(w_ref[:, :CH].T, own, NT, preferred_element_type=F32)
        queries = (queries * DH**-0.5).astype(BF)
        unit = lax.broadcasted_iota(jnp.int32, (TILE, ROWS), 0) == lax.rem(
            lax.broadcasted_iota(jnp.int32, (TILE, ROWS), 1), TILE
        )
        unit = unit.astype(F32).astype(BF)
        for h in range(HEADS):
            first, second = DH * (h % 4), DH * ((h + 1) % 4)
            stat[h, 0:TILE, :] = jnp.zeros((TILE, ROWS), BF)
            stat[h, TILE:, :] = unit
            stat[h, first : first + DH, 0:TILE] = queries[DH * h : DH * h + DH, 0:TILE]
            stat[h, second : second + DH, TILE:] = queries[DH * h : DH * h + DH, TILE:]
            for half in range(2):
                vals[half, h, 2 * DH :, :] = jnp.ones((16, vals.shape[3]), BF)
        gate_ref[...] = jax.nn.sigmoid(
            lax.dot_general(w_ref[:, 3 * CH :].T, own, NT, preferred_element_type=F32)
        )
        acc[...] = jnp.zeros_like(acc)
        mref[...] = jnp.full(mref.shape, -1e30, F32)

    first = [sum(CHUNKS[:k]) for k in range(len(CHUNKS) + 1)]

    def slots_of(chunk):
        return range(first[chunk], first[chunk + 1])

    def project_keys(chunk):
        size = CHUNKS[chunk] * TILE
        for part in range(2):
            block = got[first[chunk] : first[chunk + 1], TILE * part : TILE * part + TILE]
            block = block.reshape(size, CH)
            keys[part, 0:size] = jnp.dot(block, wk[part], preferred_element_type=F32).astype(BF)

    def project_values(chunk):
        size = CHUNKS[chunk] * TILE
        for part in range(2):
            block = got[first[chunk] : first[chunk + 1], TILE * part : TILE * part + TILE]
            block = block.reshape(size, CH)
            value = lax.dot_general(wv_t[...], block, NT, preferred_element_type=F32).astype(BF)
            for h in range(HEADS):
                vals[chunk % 2, h, DH * part : DH * part + DH, 0:size] = value[
                    DH * h : DH * h + DH
                ]

    def score(chunk, h):
        size = CHUNKS[chunk] * TILE
        lane = lax.broadcasted_iota(jnp.int32, (size, 128), 1) // DH
        lanes = slice(128 * (h // 4), 128 * (h // 4) + 128)
        key = jnp.where(lane == h % 4, keys[0, 0:size, lanes], keys[1, 0:size, lanes])
        offset = []
        for slot in slots_of(chunk):
            closed = (1 - filter_ref[res, tile_of[slot]]).astype(F32) * -1e30
            offset.append(raw[slot, h].T + closed.astype(BF))
        scores[h % 2, 0:size] = jnp.dot(
            jnp.concatenate([key, jnp.concatenate(offset, axis=0)], axis=1),
            stat[h],
            preferred_element_type=F32,
        )

    def weigh(chunk, h):
        size = CHUNKS[chunk] * TILE
        old = mref[h]
        new = jnp.maximum(old, jnp.max(scores[h % 2, 0:size], axis=0, keepdims=True))
        alpha[h] = jnp.exp(old - new)
        mref[h] = new
        probs[h % 2, 0:size] = jnp.exp(scores[h % 2, 0:size] - new[0:1]).astype(BF)

    def add(chunk, h):
        size = CHUNKS[chunk] * TILE
        acc[h] = acc[h] * alpha[h, 0:1] + jnp.dot(
            vals[chunk % 2, h, :, 0:size], probs[h % 2, 0:size], preferred_element_type=F32
        )

    work = []

    def advance(item):
        work.append(item)
        if item is not None:
            chunk, h = item
            if h == 0:
                for slot in slots_of(chunk):
                    bias_copy(slot).wait()
                project_keys(chunk)
            score(chunk, h)
            if h == 0:
                project_values(chunk)
        if len(work) > 1 and work[-2] is not None:
            weigh(*work[-2])
        if len(work) > 2:
            add(*work[-3])

    started = []
    for step in PLAN:
        if step[0] == SEND:
            copy = block_copy(*step[1:])
            copy.start()
            started.append(copy)
        elif step[0] == TAKE:
            block_copy(step[1], FROM[step[1:]], step[2]).wait_recv()
        elif step[0] == PREPARE:
            prepare()
        else:
            for h in range(step[2], step[3]):
                advance((step[1], h))
    advance(None)
    advance(None)

    attended = []
    for h in range(HEADS):
        inverse = 1.0 / acc[h, 2 * DH : 2 * DH + 1, :]
        attended.append(
            jnp.concatenate(
                [
                    acc[h, 0:DH, 0:TILE] * inverse[:, 0:TILE],
                    acc[h, DH : 2 * DH, TILE:] * inverse[:, TILE:],
                ],
                axis=1,
            )
        )
    gated = (gate_ref[...] * jnp.concatenate(attended, axis=0)).astype(BF)
    new = lax.dot_general(gated, wf_ref[...], TN, preferred_element_type=F32)
    update[...] = new.astype(BF).reshape(2, TILE, CH)

    share = TILE // SEQ

    def share_of(owner):
        return update.at[:, pl.ds(pl.multiple_of(owner * share, share), share)]

    sent = []
    for k in (4, 3, 5, 2, 6, 1, 7):
        owner = (seq + k) % SEQ
        copy = pltpu.make_async_remote_copy(
            src_ref=share_of(owner),
            dst_ref=out_ref.at[seq],
            send_sem=out_send.at[k],
            recv_sem=out_recv.at[k],
            device_id=(owner, res),
            device_id_type=MESH,
        )
        copy.start()
        sent.append(copy)
    mine = pltpu.make_async_copy(share_of(seq), out_ref.at[seq], out_recv.at[0])
    mine.start()
    for copy in started:
        copy.wait_send()
    mine.wait()
    for copy in sent:
        copy.wait()


def on_device(x, bias, allowed, gain, w, wf):
    longest = max(CHUNKS) * TILE
    out = pl.pallas_call(
        kernel,
        out_shape=jax.ShapeDtypeStruct((SEQ, 2, TILE // SEQ, CH), BF),
        in_specs=[pl.BlockSpec(memory_space=pltpu.HBM)] * 6,
        out_specs=pl.BlockSpec(memory_space=pltpu.HBM),
        scratch_shapes=[
            pltpu.VMEM((2, TILE, CH), BF),
            pltpu.SMEM((TILES, TILES), jnp.int32),
            pltpu.VMEM((1, CH), F32),
            pltpu.VMEM((CH, 4 * CH), BF),
            pltpu.VMEM((CH, CH), BF),
            pltpu.VMEM((TILES, ROWS, CH), BF),
            pltpu.VMEM((TILES, HEADS, TILE, TILE), BF),
            pltpu.VMEM((2, CH, CH), BF),
            pltpu.VMEM((CH, CH), BF),
            pltpu.VMEM((CH, ROWS), F32),
            pltpu.VMEM((2, longest, CH), BF),
            pltpu.VMEM((2, HEADS, 2 * DH + 16, longest), BF),
            pltpu.VMEM((HEADS, 2 * TILE, ROWS), BF),
            pltpu.VMEM((HEADS, 2 * DH + 16, ROWS), F32),
            pltpu.VMEM((HEADS, 8, ROWS), F32),
            pltpu.VMEM((2, longest, ROWS), F32),
            pltpu.VMEM((2, longest, ROWS), BF),
            pltpu.VMEM((HEADS, 8, ROWS), F32),
            pltpu.VMEM((2, TILE, CH), BF),
            pltpu.SemaphoreType.DMA((5,)),
            pltpu.SemaphoreType.DMA((TILES, len(PARTS))),
            pltpu.SemaphoreType.DMA((TILES, len(PARTS))),
            pltpu.SemaphoreType.DMA((TILES,)),
            pltpu.SemaphoreType.DMA((SEQ,)),
            pltpu.SemaphoreType.DMA((SEQ,)),
        ],
        compiler_params=pltpu.CompilerParams(
            collective_id=0, has_side_effects=True, vmem_limit_bytes=63 * 2**20
        ),
        cost_estimate=pl.CostEstimate(
            flops=4 * 2**30, bytes_accessed=9 * 2**20, transcendentals=2**23
        ),
    )(x, bias, allowed, gain.reshape(1, CH), w, wf)
    return jnp.transpose(out.reshape(2 * SEQ, TILE // SEQ, CH), (1, 0, 2))


def solution(mesh):
    return jax.shard_map(
        on_device,
        mesh=mesh,
        in_specs=(P("seq", "res", None), P(None, "res", None), P(), P(), P(), P()),
        out_specs=P(("res", "seq"), None, None),
        check_vma=False,
    )
```

```python
import jax
import jax.numpy as jnp
from jax import lax
from jax.experimental import pallas as pl
from jax.experimental.pallas import tpu as pltpu
from jax.sharding import PartitionSpec as P

NY, NZ = 4, 8
TILES = NY * NZ
SEQ = 8
HEADS, DH, TILE, CH = 8, 32, 128, 256
ROWS = 2 * TILE
PARTS = (112, 80, 64)
CHUNKS = (3, 3, 4, 3, 3, 3, 4, 3, 4, 2)
MESH = pl.DeviceIdType.MESH
BF, F32 = jnp.bfloat16, jnp.float32
NT = (((1,), (1,)), ((), ()))
TN = (((0,), (0,)), ((), ()))

SLOTS = (
    (0, 0), (1, 0), (-1, 0), (0, 1), (0, -1), (-1, -1), (1, 1), (-1, 1), (2, 0), (0, 2), (0, -2), (-1, -2),
    (1, -1), (2, 1), (-1, 2), (1, -2), (0, 3), (2, -1), (2, 2), (-1, -3), (0, -3), (1, 2), (1, -3), (-1, 3),
    (2, -2), (-1, 4), (0, 4), (2, 3), (1, 4), (1, 3), (2, 4), (2, -3),
)

SEND, TAKE, PREPARE, ATTEND = range(4)
PLAN = (
    (0, 0, 0, 1), (0, 0, 0, 2), (0, 1, 0, 3), (0, 2, 0, 4), (2,), (0, 2, 0, 1), (0, 1, 0, 2), (0, 2, 0, 3),
    (0, 1, 0, 4), (0, 1, 0, 1), (0, 0, 0, 3), (0, 2, 0, 2), (0, 0, 0, 4), (1, 2, 4), (0, 2, 4, 12),
    (0, 2, 4, 5), (0, 2, 4, 10), (1, 1, 3), (0, 1, 3, 9), (0, 1, 3, 6), (0, 1, 3, 7), (1, 0, 1), (1, 0, 2),
    (0, 0, 2, 5), (0, 0, 1, 6), (0, 0, 1, 8), (1, 2, 1), (1, 2, 3), (0, 2, 3, 7), (1, 1, 2), (1, 1, 4),
    (0, 1, 4, 10), (0, 2, 3, 9), (0, 1, 4, 5), (1, 1, 1), (1, 2, 2), (0, 2, 3, 6), (0, 2, 2, 8), (0, 0, 2, 7),
    (0, 0, 1, 12), (0, 1, 1, 8), (3, 0, 0, 8), (1, 0, 3), (1, 0, 4), (1, 2, 12), (1, 2, 5), (1, 2, 10),
    (1, 1, 9), (0, 2, 12, 17), (0, 2, 10, 11), (0, 0, 3, 9), (0, 2, 10, 20), (1, 1, 6), (1, 1, 7),
    (0, 1, 7, 13), (0, 0, 4, 10), (0, 2, 10, 15), (1, 0, 5), (1, 0, 6), (1, 2, 7), (0, 1, 9, 16),
    (0, 1, 9, 14), (1, 0, 8), (0, 1, 9, 21), (1, 2, 9), (1, 1, 10), (0, 0, 5, 11), (1, 1, 5), (0, 1, 10, 15),
    (0, 1, 10, 11), (0, 0, 8, 13), (0, 1, 10, 20), (0, 1, 4, 12), (0, 2, 9, 14), (0, 2, 9, 16), (3, 1, 0, 8),
    (1, 2, 6), (1, 2, 8), (1, 0, 7), (1, 0, 12), (1, 1, 8), (1, 2, 11), (1, 2, 20), (1, 2, 17),
    (0, 2, 20, 19), (0, 0, 7, 14), (0, 0, 12, 15), (1, 0, 9), (0, 2, 6, 13), (0, 2, 20, 22), (0, 2, 11, 24),
    (0, 0, 9, 16), (0, 2, 20, 26), (0, 2, 9, 21), (0, 1, 5, 17), (0, 0, 8, 17), (3, 2, 0, 8), (1, 1, 13),
    (1, 2, 15), (1, 0, 10), (1, 1, 16), (1, 1, 14), (1, 1, 21), (1, 0, 11), (1, 1, 11), (1, 0, 13),
    (1, 1, 15), (0, 1, 16, 29), (0, 1, 16, 23), (0, 0, 13, 18), (1, 2, 14), (1, 2, 16), (1, 1, 20),
    (0, 2, 16, 23), (0, 1, 20, 22), (0, 0, 11, 19), (1, 1, 12), (0, 1, 21, 18), (0, 2, 14, 18),
    (0, 1, 16, 26), (0, 0, 10, 20), (0, 1, 20, 19), (0, 0, 6, 21), (0, 2, 16, 29), (3, 3, 0, 8), (1, 2, 19),
    (1, 2, 13), (1, 0, 14), (1, 0, 15), (1, 2, 24), (1, 2, 22), (1, 2, 26), (1, 1, 17), (1, 2, 21),
    (0, 2, 26, 28), (0, 2, 26, 25), (0, 0, 14, 23), (0, 0, 15, 22), (0, 2, 22, 31), (3, 4, 0, 8), (1, 0, 16),
    (1, 1, 23), (1, 1, 29), (1, 0, 17), (1, 0, 18), (1, 2, 23), (1, 1, 22), (0, 1, 15, 24), (0, 1, 23, 27),
    (0, 0, 18, 27), (0, 0, 17, 24), (1, 0, 19), (1, 2, 18), (1, 1, 26), (0, 1, 26, 25), (1, 1, 18),
    (0, 1, 26, 28), (0, 0, 16, 26), (0, 0, 19, 25), (3, 5, 0, 8), (1, 1, 19), (1, 2, 29), (1, 0, 20),
    (1, 0, 21), (1, 2, 25), (1, 2, 28), (0, 2, 29, 27), (0, 1, 19, 31), (0, 0, 21, 29), (1, 0, 22),
    (0, 0, 22, 28), (0, 2, 25, 30), (3, 6, 0, 8), (1, 0, 23), (1, 2, 31), (1, 1, 27), (1, 1, 24), (1, 0, 24),
    (1, 0, 27), (1, 1, 25), (1, 1, 28), (0, 1, 28, 30), (0, 0, 27, 30), (0, 0, 24, 31), (1, 0, 25),
    (3, 7, 0, 8), (1, 0, 26), (1, 2, 27), (1, 1, 31), (1, 0, 28), (1, 0, 29), (1, 2, 30), (3, 8, 0, 8),
    (1, 1, 30), (1, 0, 30), (1, 0, 31), (3, 9, 0, 8),
)


def way_of(source, target):
    dy = (SLOTS[target][0] - SLOTS[source][0]) % NY
    dz = (SLOTS[target][1] - SLOTS[source][1]) % NZ
    return ("y", 1 if dy == 1 else -1) if dy else ("z", 1 if dz == 1 else -1)


FROM = {(step[1], step[3]): step[2] for step in PLAN if step[0] == SEND}


def kernel(
    x_hbm, bias_ref, filter_hbm, gain_hbm, w_hbm, wf_hbm, out_ref,
    x_ref, filter_ref, gain_ref, w_ref, wf_ref, got, raw, wk, wv_t, gate_ref, keys, vals, stat, acc, mref, scores, probs, alpha, update,
    load_sem, send_sem, recv_sem, bias_sem, out_send, out_recv,
):
    seq, res = lax.axis_index("seq"), lax.axis_index("res")
    y, z = res // NZ, res % NZ
    near = {
        ("z", 1): y * NZ + (z + 1) % NZ,
        ("z", -1): y * NZ + (z + NZ - 1) % NZ,
        ("y", 1): ((y + 1) % NY) * NZ + z,
        ("y", -1): ((y + NY - 1) % NY) * NZ + z,
    }
    barrier = pltpu.get_barrier_semaphore()
    for other in near.values():
        pl.semaphore_signal(barrier, inc=1, device_id=(seq, other), device_id_type=MESH)
    for k in range(1, SEQ):
        pl.semaphore_signal(barrier, inc=1, device_id=((seq + k) % SEQ, res), device_id_type=MESH)

    loads = [
        pltpu.make_async_copy(source, target, load_sem.at[k])
        for k, (source, target) in enumerate(
            (
                (x_hbm, x_ref),
                (gain_hbm, gain_ref),
                (w_hbm, w_ref),
                (wf_hbm, wf_ref),
                (filter_hbm, filter_ref),
            )
        )
    ]
    for load in loads:
        load.start()
    tile_of = [((y + NY - dy) % NY) * NZ + (z + NZ - dz) % NZ for dy, dz in SLOTS]

    def bias_copy(slot):
        columns = pl.ds(pl.multiple_of(tile_of[slot] * TILE, TILE), TILE)
        return pltpu.make_async_copy(bias_ref.at[:, :, columns], raw.at[slot], bias_sem.at[slot])

    loads[0].wait()
    loads[1].wait()
    rows = x_ref[...].reshape(ROWS, CH).astype(F32)
    rows = rows - jnp.mean(rows, axis=-1, keepdims=True)
    variance = jnp.mean(rows * rows, axis=-1, keepdims=True)
    own = (rows * lax.rsqrt(variance + 1e-5) * gain_ref[...]).astype(BF)
    got[0] = own

    pl.semaphore_wait(barrier, 4 + SEQ - 1)
    part_rows = [pl.ds(sum(PARTS[:k]), PARTS[k]) for k in range(len(PARTS))]

    def block_copy(part, source, target):
        return pltpu.make_async_remote_copy(
            src_ref=got.at[source, part_rows[part]],
            dst_ref=got.at[target, part_rows[part]],
            send_sem=send_sem.at[target, part],
            recv_sem=recv_sem.at[target, part],
            device_id=(seq, near[way_of(source, target)]),
            device_id_type=MESH,
        )

    def prepare():
        for slot in range(TILES):
            bias_copy(slot).start()
        for load in loads[2:]:
            load.wait()
        for part in range(2):
            for group in range(2):
                lanes = pl.ds(CH + 128 * group, 128)
                w = w_ref[:, lanes]
                if part == 1:
                    w = pltpu.roll(w.astype(F32), DH, 1).astype(BF)
                wk[part, :, 128 * group : 128 * group + 128] = w
        wv_t[...] = w_ref[:, 2 * CH : 3 * CH].T
        queries = lax.dot_general(w_ref[:, :CH].T, own, NT, preferred_element_type=F32)
        queries = (queries * DH**-0.5).astype(BF)
        unit = lax.broadcasted_iota(jnp.int32, (TILE, ROWS), 0) == lax.rem(
            lax.broadcasted_iota(jnp.int32, (TILE, ROWS), 1), TILE
        )
        unit = unit.astype(F32).astype(BF)
        for h in range(HEADS):
            first, second = DH * (h % 4), DH * ((h + 1) % 4)
            stat[h, 0:TILE, :] = jnp.zeros((TILE, ROWS), BF)
            stat[h, TILE:, :] = unit
            stat[h, first : first + DH, 0:TILE] = queries[DH * h : DH * h + DH, 0:TILE]
            stat[h, second : second + DH, TILE:] = queries[DH * h : DH * h + DH, TILE:]
            for half in range(2):
                vals[half, h, 2 * DH :, :] = jnp.ones((16, vals.shape[3]), BF)
        gate_ref[...] = jax.nn.sigmoid(
            lax.dot_general(w_ref[:, 3 * CH :].T, own, NT, preferred_element_type=F32)
        )
        acc[...] = jnp.zeros_like(acc)
        mref[...] = jnp.full(mref.shape, -1e30, F32)

    first = [sum(CHUNKS[:k]) for k in range(len(CHUNKS) + 1)]

    def slots_of(chunk):
        return range(first[chunk], first[chunk + 1])

    def project_keys(chunk):
        size = CHUNKS[chunk] * TILE
        for part in range(2):
            block = got[first[chunk] : first[chunk + 1], TILE * part : TILE * part + TILE]
            block = block.reshape(size, CH)
            keys[part, 0:size] = jnp.dot(block, wk[part], preferred_element_type=F32).astype(BF)

    def project_values(chunk):
        size = CHUNKS[chunk] * TILE
        for part in range(2):
            block = got[first[chunk] : first[chunk + 1], TILE * part : TILE * part + TILE]
            block = block.reshape(size, CH)
            value = lax.dot_general(wv_t[...], block, NT, preferred_element_type=F32).astype(BF)
            for h in range(HEADS):
                vals[chunk % 2, h, DH * part : DH * part + DH, 0:size] = value[
                    DH * h : DH * h + DH
                ]

    def score(chunk, h):
        size = CHUNKS[chunk] * TILE
        lane = lax.broadcasted_iota(jnp.int32, (size, 128), 1) // DH
        lanes = slice(128 * (h // 4), 128 * (h // 4) + 128)
        key = jnp.where(lane == h % 4, keys[0, 0:size, lanes], keys[1, 0:size, lanes])
        offset = []
        for slot in slots_of(chunk):
            closed = (1 - filter_ref[res, tile_of[slot]]).astype(F32) * -1e30
            offset.append(raw[slot, h].T + closed.astype(BF))
        scores[h % 2, 0:size] = jnp.dot(
            jnp.concatenate([key, jnp.concatenate(offset, axis=0)], axis=1),
            stat[h],
            preferred_element_type=F32,
        )

    def weigh(chunk, h):
        size = CHUNKS[chunk] * TILE
        old = mref[h]
        new = jnp.maximum(old, jnp.max(scores[h % 2, 0:size], axis=0, keepdims=True))
        alpha[h] = jnp.exp(old - new)
        mref[h] = new
        probs[h % 2, 0:size] = jnp.exp(scores[h % 2, 0:size] - new[0:1]).astype(BF)

    def add(chunk, h):
        size = CHUNKS[chunk] * TILE
        acc[h] = acc[h] * alpha[h, 0:1] + jnp.dot(
            vals[chunk % 2, h, :, 0:size], probs[h % 2, 0:size], preferred_element_type=F32
        )

    work = []

    def advance(item):
        work.append(item)
        if item is not None:
            chunk, h = item
            if h == 0:
                for slot in slots_of(chunk):
                    bias_copy(slot).wait()
                project_keys(chunk)
            score(chunk, h)
            if h == 0:
                project_values(chunk)
        if len(work) > 1 and work[-2] is not None:
            weigh(*work[-2])
        if len(work) > 2:
            add(*work[-3])

    started = []
    for step in PLAN:
        if step[0] == SEND:
            copy = block_copy(*step[1:])
            copy.start()
            started.append(copy)
        elif step[0] == TAKE:
            block_copy(step[1], FROM[step[1:]], step[2]).wait_recv()
        elif step[0] == PREPARE:
            prepare()
        else:
            for h in range(step[2], step[3]):
                advance((step[1], h))
    advance(None)
    advance(None)

    attended = []
    for h in range(HEADS):
        inverse = 1.0 / acc[h, 2 * DH : 2 * DH + 1, :]
        attended.append(
            jnp.concatenate(
                [
                    acc[h, 0:DH, 0:TILE] * inverse[:, 0:TILE],
                    acc[h, DH : 2 * DH, TILE:] * inverse[:, TILE:],
                ],
                axis=1,
            )
        )
    gated = (gate_ref[...] * jnp.concatenate(attended, axis=0)).astype(BF)
    new = lax.dot_general(gated, wf_ref[...], TN, preferred_element_type=F32)
    update[...] = new.astype(BF).reshape(2, TILE, CH)

    share = TILE // SEQ

    def share_of(owner):
        return update.at[:, pl.ds(pl.multiple_of(owner * share, share), share)]

    sent = []
    for k in (4, 3, 5, 2, 6, 1, 7):
        owner = (seq + k) % SEQ
        copy = pltpu.make_async_remote_copy(
            src_ref=share_of(owner),
            dst_ref=out_ref.at[seq],
            send_sem=out_send.at[k],
            recv_sem=out_recv.at[k],
            device_id=(owner, res),
            device_id_type=MESH,
        )
        copy.start()
        sent.append(copy)
    mine = pltpu.make_async_copy(share_of(seq), out_ref.at[seq], out_recv.at[0])
    mine.start()
    for copy in started:
        copy.wait_send()
    mine.wait()
    for copy in sent:
        copy.wait()


def on_device(x, bias, allowed, gain, w, wf):
    longest = max(CHUNKS) * TILE
    out = pl.pallas_call(
        kernel,
        out_shape=jax.ShapeDtypeStruct((SEQ, 2, TILE // SEQ, CH), BF),
        in_specs=[pl.BlockSpec(memory_space=pltpu.HBM)] * 6,
        out_specs=pl.BlockSpec(memory_space=pltpu.HBM),
        scratch_shapes=[
            pltpu.VMEM((2, TILE, CH), BF),
            pltpu.SMEM((TILES, TILES), jnp.int32),
            pltpu.VMEM((1, CH), F32),
            pltpu.VMEM((CH, 4 * CH), BF),
            pltpu.VMEM((CH, CH), BF),
            pltpu.VMEM((TILES, ROWS, CH), BF),
            pltpu.VMEM((TILES, HEADS, TILE, TILE), BF),
            pltpu.VMEM((2, CH, CH), BF),
            pltpu.VMEM((CH, CH), BF),
            pltpu.VMEM((CH, ROWS), F32),
            pltpu.VMEM((2, longest, CH), BF),
            pltpu.VMEM((2, HEADS, 2 * DH + 16, longest), BF),
            pltpu.VMEM((HEADS, 2 * TILE, ROWS), BF),
            pltpu.VMEM((HEADS, 2 * DH + 16, ROWS), F32),
            pltpu.VMEM((HEADS, 8, ROWS), F32),
            pltpu.VMEM((2, longest, ROWS), F32),
            pltpu.VMEM((2, longest, ROWS), BF),
            pltpu.VMEM((HEADS, 8, ROWS), F32),
            pltpu.VMEM((2, TILE, CH), BF),
            pltpu.SemaphoreType.DMA((5,)),
            pltpu.SemaphoreType.DMA((TILES, len(PARTS))),
            pltpu.SemaphoreType.DMA((TILES, len(PARTS))),
            pltpu.SemaphoreType.DMA((TILES,)),
            pltpu.SemaphoreType.DMA((SEQ,)),
            pltpu.SemaphoreType.DMA((SEQ,)),
        ],
        compiler_params=pltpu.CompilerParams(
            collective_id=0, has_side_effects=True, vmem_limit_bytes=63 * 2**20
        ),
        cost_estimate=pl.CostEstimate(
            flops=4 * 2**30, bytes_accessed=9 * 2**20, transcendentals=2**23
        ),
    )(x, bias, allowed, gain.reshape(1, CH), w, wf)
    return jnp.transpose(out.reshape(2 * SEQ, TILE // SEQ, CH), (1, 0, 2))


def solution(mesh):
    return jax.shard_map(
        on_device,
        mesh=mesh,
        in_specs=(P("seq", "res", None), P(None, "res", None), P(), P(), P(), P()),
        out_specs=P(("res", "seq"), None, None),
        check_vma=False,
    )
```

```python
import jax
import jax.numpy as jnp
from jax import lax
from jax.experimental import pallas as pl
from jax.experimental.pallas import tpu as pltpu
from jax.sharding import PartitionSpec as P

NY, NZ = 4, 8
TILES = NY * NZ
SEQ = 8
HEADS, DH, TILE, CH = 8, 32, 128, 256
ROWS = 2 * TILE
PARTS = (112, 80, 64)
CHUNKS = (3, 3, 4, 3, 3, 3, 4, 3, 4, 2)
MESH = pl.DeviceIdType.MESH
BF, F32 = jnp.bfloat16, jnp.float32
NT = (((1,), (1,)), ((), ()))
TN = (((0,), (0,)), ((), ()))

SLOTS = (
    (0, 0), (1, 0), (-1, 0), (0, 1), (0, -1), (-1, -1), (1, 1), (-1, 1), (2, 0), (0, 2), (0, -2), (-1, -2),
    (1, -1), (2, 1), (-1, 2), (1, -2), (0, 3), (2, -1), (2, 2), (-1, -3), (0, -3), (1, 2), (1, -3), (-1, 3),
    (2, -2), (-1, 4), (0, 4), (2, 3), (1, 4), (1, 3), (2, 4), (2, -3),
)

SEND, TAKE, PREPARE, ATTEND = range(4)
PLAN = (
    (0, 0, 0, 1), (0, 0, 0, 2), (0, 1, 0, 3), (0, 2, 0, 4), (2,), (0, 2, 0, 1), (0, 1, 0, 2), (0, 2, 0, 3),
    (0, 1, 0, 4), (0, 1, 0, 1), (0, 0, 0, 3), (0, 2, 0, 2), (0, 0, 0, 4), (1, 2, 4), (0, 2, 4, 12),
    (0, 2, 4, 5), (0, 2, 4, 10), (1, 1, 3), (0, 1, 3, 9), (0, 1, 3, 6), (0, 1, 3, 7), (1, 0, 1), (1, 0, 2),
    (0, 0, 2, 5), (0, 0, 1, 6), (0, 0, 1, 8), (1, 2, 1), (1, 2, 3), (0, 2, 3, 7), (1, 1, 2), (1, 1, 4),
    (0, 1, 4, 10), (0, 2, 3, 9), (0, 1, 4, 5), (1, 1, 1), (1, 2, 2), (0, 2, 3, 6), (0, 2, 2, 8), (0, 0, 2, 7),
    (0, 0, 1, 12), (0, 1, 1, 8), (3, 0, 0, 8), (1, 0, 3), (1, 0, 4), (1, 2, 12), (1, 2, 5), (1, 2, 10),
    (1, 1, 9), (0, 2, 12, 17), (0, 2, 10, 11), (0, 0, 3, 9), (0, 2, 10, 20), (1, 1, 6), (1, 1, 7),
    (0, 1, 7, 13), (0, 0, 4, 10), (0, 2, 10, 15), (1, 0, 5), (1, 0, 6), (1, 2, 7), (0, 1, 9, 16),
    (0, 1, 9, 14), (1, 0, 8), (0, 1, 9, 21), (1, 2, 9), (1, 1, 10), (0, 0, 5, 11), (1, 1, 5), (0, 1, 10, 15),
    (0, 1, 10, 11), (0, 0, 8, 13), (0, 1, 10, 20), (0, 1, 4, 12), (0, 2, 9, 14), (0, 2, 9, 16), (3, 1, 0, 8),
    (1, 2, 6), (1, 2, 8), (1, 0, 7), (1, 0, 12), (1, 1, 8), (1, 2, 11), (1, 2, 20), (1, 2, 17),
    (0, 2, 20, 19), (0, 0, 7, 14), (0, 0, 12, 15), (1, 0, 9), (0, 2, 6, 13), (0, 2, 20, 22), (0, 2, 11, 24),
    (0, 0, 9, 16), (0, 2, 20, 26), (0, 2, 9, 21), (0, 1, 5, 17), (0, 0, 8, 17), (3, 2, 0, 8), (1, 1, 13),
    (1, 2, 15), (1, 0, 10), (1, 1, 16), (1, 1, 14), (1, 1, 21), (1, 0, 11), (1, 1, 11), (1, 0, 13),
    (1, 1, 15), (0, 1, 16, 29), (0, 1, 16, 23), (0, 0, 13, 18), (1, 2, 14), (1, 2, 16), (1, 1, 20),
    (0, 2, 16, 23), (0, 1, 20, 22), (0, 0, 11, 19), (1, 1, 12), (0, 1, 21, 18), (0, 2, 14, 18),
    (0, 1, 16, 26), (0, 0, 10, 20), (0, 1, 20, 19), (0, 0, 6, 21), (0, 2, 16, 29), (3, 3, 0, 8), (1, 2, 19),
    (1, 2, 13), (1, 0, 14), (1, 0, 15), (1, 2, 24), (1, 2, 22), (1, 2, 26), (1, 1, 17), (1, 2, 21),
    (0, 2, 26, 28), (0, 2, 26, 25), (0, 0, 14, 23), (0, 0, 15, 22), (0, 2, 22, 31), (3, 4, 0, 8), (1, 0, 16),
    (1, 1, 23), (1, 1, 29), (1, 0, 17), (1, 0, 18), (1, 2, 23), (1, 1, 22), (0, 1, 15, 24), (0, 1, 23, 27),
    (0, 0, 18, 27), (0, 0, 17, 24), (1, 0, 19), (1, 2, 18), (1, 1, 26), (0, 1, 26, 25), (1, 1, 18),
    (0, 1, 26, 28), (0, 0, 16, 26), (0, 0, 19, 25), (3, 5, 0, 8), (1, 1, 19), (1, 2, 29), (1, 0, 20),
    (1, 0, 21), (1, 2, 25), (1, 2, 28), (0, 2, 29, 27), (0, 1, 19, 31), (0, 0, 21, 29), (1, 0, 22),
    (0, 0, 22, 28), (0, 2, 25, 30), (3, 6, 0, 8), (1, 0, 23), (1, 2, 31), (1, 1, 27), (1, 1, 24), (1, 0, 24),
    (1, 0, 27), (1, 1, 25), (1, 1, 28), (0, 1, 28, 30), (0, 0, 27, 30), (0, 0, 24, 31), (1, 0, 25),
    (3, 7, 0, 8), (1, 0, 26), (1, 2, 27), (1, 1, 31), (1, 0, 28), (1, 0, 29), (1, 2, 30), (3, 8, 0, 8),
    (1, 1, 30), (1, 0, 30), (1, 0, 31), (3, 9, 0, 8),
)


def way_of(source, target):
    dy = (SLOTS[target][0] - SLOTS[source][0]) % NY
    dz = (SLOTS[target][1] - SLOTS[source][1]) % NZ
    return ("y", 1 if dy == 1 else -1) if dy else ("z", 1 if dz == 1 else -1)


FROM = {(step[1], step[3]): step[2] for step in PLAN if step[0] == SEND}


def kernel(
    x_hbm, bias_ref, filter_hbm, gain_hbm, w_hbm, wf_hbm, out_ref,
    x_ref, filter_ref, gain_ref, w_ref, wf_ref, got, raw, wk, wv_t, gate_ref, keys, vals, stat, acc, mref, scores, probs, alpha, update,
    load_sem, send_sem, recv_sem, bias_sem, out_send, out_recv,
):
    seq, res = lax.axis_index("seq"), lax.axis_index("res")
    y, z = res // NZ, res % NZ
    near = {
        ("z", 1): y * NZ + (z + 1) % NZ,
        ("z", -1): y * NZ + (z + NZ - 1) % NZ,
        ("y", 1): ((y + 1) % NY) * NZ + z,
        ("y", -1): ((y + NY - 1) % NY) * NZ + z,
    }
    barrier = pltpu.get_barrier_semaphore()
    for other in near.values():
        pl.semaphore_signal(barrier, inc=1, device_id=(seq, other), device_id_type=MESH)
    for k in range(1, SEQ):
        pl.semaphore_signal(barrier, inc=1, device_id=((seq + k) % SEQ, res), device_id_type=MESH)

    loads = [
        pltpu.make_async_copy(source, target, load_sem.at[k])
        for k, (source, target) in enumerate(
            (
                (x_hbm, x_ref),
                (gain_hbm, gain_ref),
                (w_hbm, w_ref),
                (wf_hbm, wf_ref),
                (filter_hbm, filter_ref),
            )
        )
    ]
    for load in loads:
        load.start()
    tile_of = [((y + NY - dy) % NY) * NZ + (z + NZ - dz) % NZ for dy, dz in SLOTS]

    def bias_copy(slot):
        columns = pl.ds(pl.multiple_of(tile_of[slot] * TILE, TILE), TILE)
        return pltpu.make_async_copy(bias_ref.at[:, :, columns], raw.at[slot], bias_sem.at[slot])

    loads[0].wait()
    loads[1].wait()
    rows = x_ref[...].reshape(ROWS, CH).astype(F32)
    rows = rows - jnp.mean(rows, axis=-1, keepdims=True)
    variance = jnp.mean(rows * rows, axis=-1, keepdims=True)
    own = (rows * lax.rsqrt(variance + 1e-5) * gain_ref[...]).astype(BF)
    got[0] = own

    pl.semaphore_wait(barrier, 4 + SEQ - 1)
    part_rows = [pl.ds(sum(PARTS[:k]), PARTS[k]) for k in range(len(PARTS))]

    def block_copy(part, source, target):
        return pltpu.make_async_remote_copy(
            src_ref=got.at[source, part_rows[part]],
            dst_ref=got.at[target, part_rows[part]],
            send_sem=send_sem.at[target, part],
            recv_sem=recv_sem.at[target, part],
            device_id=(seq, near[way_of(source, target)]),
            device_id_type=MESH,
        )

    def prepare():
        for slot in range(TILES):
            bias_copy(slot).start()
        for load in loads[2:]:
            load.wait()
        for part in range(2):
            for group in range(2):
                lanes = pl.ds(CH + 128 * group, 128)
                w = w_ref[:, lanes]
                if part == 1:
                    w = pltpu.roll(w.astype(F32), DH, 1).astype(BF)
                wk[part, :, 128 * group : 128 * group + 128] = w
        wv_t[...] = w_ref[:, 2 * CH : 3 * CH].T
        queries = lax.dot_general(w_ref[:, :CH].T, own, NT, preferred_element_type=F32)
        queries = (queries * DH**-0.5).astype(BF)
        unit = lax.broadcasted_iota(jnp.int32, (TILE, ROWS), 0) == lax.rem(
            lax.broadcasted_iota(jnp.int32, (TILE, ROWS), 1), TILE
        )
        unit = unit.astype(F32).astype(BF)
        for h in range(HEADS):
            first, second = DH * (h % 4), DH * ((h + 1) % 4)
            stat[h, 0:TILE, :] = jnp.zeros((TILE, ROWS), BF)
            stat[h, TILE:, :] = unit
            stat[h, first : first + DH, 0:TILE] = queries[DH * h : DH * h + DH, 0:TILE]
            stat[h, second : second + DH, TILE:] = queries[DH * h : DH * h + DH, TILE:]
            for half in range(2):
                vals[half, h, 2 * DH :, :] = jnp.ones((16, vals.shape[3]), BF)
        gate_ref[...] = jax.nn.sigmoid(
            lax.dot_general(w_ref[:, 3 * CH :].T, own, NT, preferred_element_type=F32)
        )
        acc[...] = jnp.zeros_like(acc)
        mref[...] = jnp.full(mref.shape, -1e30, F32)

    first = [sum(CHUNKS[:k]) for k in range(len(CHUNKS) + 1)]

    def slots_of(chunk):
        return range(first[chunk], first[chunk + 1])

    def project_keys(chunk):
        size = CHUNKS[chunk] * TILE
        for part in range(2):
            block = got[first[chunk] : first[chunk + 1], TILE * part : TILE * part + TILE]
            block = block.reshape(size, CH)
            keys[part, 0:size] = jnp.dot(block, wk[part], preferred_element_type=F32).astype(BF)

    def project_values(chunk):
        size = CHUNKS[chunk] * TILE
        for part in range(2):
            block = got[first[chunk] : first[chunk + 1], TILE * part : TILE * part + TILE]
            block = block.reshape(size, CH)
            value = lax.dot_general(wv_t[...], block, NT, preferred_element_type=F32).astype(BF)
            for h in range(HEADS):
                vals[chunk % 2, h, DH * part : DH * part + DH, 0:size] = value[
                    DH * h : DH * h + DH
                ]

    def score(chunk, h):
        size = CHUNKS[chunk] * TILE
        lane = lax.broadcasted_iota(jnp.int32, (size, 128), 1) // DH
        lanes = slice(128 * (h // 4), 128 * (h // 4) + 128)
        key = jnp.where(lane == h % 4, keys[0, 0:size, lanes], keys[1, 0:size, lanes])
        offset = []
        for slot in slots_of(chunk):
            closed = (1 - filter_ref[res, tile_of[slot]]).astype(F32) * -1e30
            offset.append(raw[slot, h].T + closed.astype(BF))
        scores[h % 2, 0:size] = jnp.dot(
            jnp.concatenate([key, jnp.concatenate(offset, axis=0)], axis=1),
            stat[h],
            preferred_element_type=F32,
        )

    def weigh(chunk, h):
        size = CHUNKS[chunk] * TILE
        old = mref[h]
        new = jnp.maximum(old, jnp.max(scores[h % 2, 0:size], axis=0, keepdims=True))
        alpha[h] = jnp.exp(old - new)
        mref[h] = new
        probs[h % 2, 0:size] = jnp.exp(scores[h % 2, 0:size] - new[0:1]).astype(BF)

    def add(chunk, h):
        size = CHUNKS[chunk] * TILE
        acc[h] = acc[h] * alpha[h, 0:1] + jnp.dot(
            vals[chunk % 2, h, :, 0:size], probs[h % 2, 0:size], preferred_element_type=F32
        )

    work = []

    def advance(item):
        work.append(item)
        if item is not None:
            chunk, h = item
            if h == 0:
                for slot in slots_of(chunk):
                    bias_copy(slot).wait()
                project_keys(chunk)
            score(chunk, h)
            if h == 0:
                project_values(chunk)
        if len(work) > 1 and work[-2] is not None:
            weigh(*work[-2])
        if len(work) > 2:
            add(*work[-3])

    started = []
    for step in PLAN:
        if step[0] == SEND:
            copy = block_copy(*step[1:])
            copy.start()
            started.append(copy)
        elif step[0] == TAKE:
            block_copy(step[1], FROM[step[1:]], step[2]).wait_recv()
        elif step[0] == PREPARE:
            prepare()
        else:
            for h in range(step[2], step[3]):
                advance((step[1], h))
    advance(None)
    advance(None)

    share = TILE // SEQ
    sent, mine = [], []
    for part in range(2):
        lanes = slice(TILE * part, TILE * part + TILE)
        attended = [
            acc[h, DH * part : DH * part + DH, lanes] * (1.0 / acc[h, 2 * DH : 2 * DH + 1, lanes])
            for h in range(HEADS)
        ]
        gated = (gate_ref[:, lanes] * jnp.concatenate(attended, axis=0)).astype(BF)
        new = lax.dot_general(gated, wf_ref[...], TN, preferred_element_type=F32)
        update[part] = new.astype(BF)

        def share_of(owner):
            return update.at[part, pl.ds(pl.multiple_of(owner * share, share), share)]

        for k in (4, 3, 5, 2, 6, 1, 7):
            owner = (seq + k) % SEQ
            copy = pltpu.make_async_remote_copy(
                src_ref=share_of(owner),
                dst_ref=out_ref.at[seq, part],
                send_sem=out_send.at[k, part],
                recv_sem=out_recv.at[k, part],
                device_id=(owner, res),
                device_id_type=MESH,
            )
            copy.start()
            sent.append(copy)
        mine.append(
            pltpu.make_async_copy(share_of(seq), out_ref.at[seq, part], out_recv.at[0, part])
        )
        mine[part].start()
    for copy in started:
        copy.wait_send()
    for copy in mine:
        copy.wait()
    for copy in sent:
        copy.wait()


def on_device(x, bias, allowed, gain, w, wf):
    longest = max(CHUNKS) * TILE
    out = pl.pallas_call(
        kernel,
        out_shape=jax.ShapeDtypeStruct((SEQ, 2, TILE // SEQ, CH), BF),
        in_specs=[pl.BlockSpec(memory_space=pltpu.HBM)] * 6,
        out_specs=pl.BlockSpec(memory_space=pltpu.HBM),
        scratch_shapes=[
            pltpu.VMEM((2, TILE, CH), BF),
            pltpu.SMEM((TILES, TILES), jnp.int32),
            pltpu.VMEM((1, CH), F32),
            pltpu.VMEM((CH, 4 * CH), BF),
            pltpu.VMEM((CH, CH), BF),
            pltpu.VMEM((TILES, ROWS, CH), BF),
            pltpu.VMEM((TILES, HEADS, TILE, TILE), BF),
            pltpu.VMEM((2, CH, CH), BF),
            pltpu.VMEM((CH, CH), BF),
            pltpu.VMEM((CH, ROWS), F32),
            pltpu.VMEM((2, longest, CH), BF),
            pltpu.VMEM((2, HEADS, 2 * DH + 16, longest), BF),
            pltpu.VMEM((HEADS, 2 * TILE, ROWS), BF),
            pltpu.VMEM((HEADS, 2 * DH + 16, ROWS), F32),
            pltpu.VMEM((HEADS, 8, ROWS), F32),
            pltpu.VMEM((2, longest, ROWS), F32),
            pltpu.VMEM((2, longest, ROWS), BF),
            pltpu.VMEM((HEADS, 8, ROWS), F32),
            pltpu.VMEM((2, TILE, CH), BF),
            pltpu.SemaphoreType.DMA((5,)),
            pltpu.SemaphoreType.DMA((TILES, len(PARTS))),
            pltpu.SemaphoreType.DMA((TILES, len(PARTS))),
            pltpu.SemaphoreType.DMA((TILES,)),
            pltpu.SemaphoreType.DMA((SEQ, 2)),
            pltpu.SemaphoreType.DMA((SEQ, 2)),
        ],
        compiler_params=pltpu.CompilerParams(
            collective_id=0, has_side_effects=True, vmem_limit_bytes=63 * 2**20
        ),
        cost_estimate=pl.CostEstimate(
            flops=4 * 2**30, bytes_accessed=9 * 2**20, transcendentals=2**23
        ),
    )(x, bias, allowed, gain.reshape(1, CH), w, wf)
    return jnp.transpose(out.reshape(2 * SEQ, TILE // SEQ, CH), (1, 0, 2))


def solution(mesh):
    return jax.shard_map(
        on_device,
        mesh=mesh,
        in_specs=(P("seq", "res", None), P(None, "res", None), P(), P(), P(), P()),
        out_specs=P(("res", "seq"), None, None),
        check_vma=False,
    )
```
